32 devices in a mesh: seq: 8 (over y, x, core), dp: 4 (over z).
Axes of the slice: x: 2, y: 2, z: 4, core: 2. Of those that a mesh axis runs over, the one named last changes fastest.
Arguments:
- layer_input: bfloat16 [4, 2048, 4096], P('dp', None, 'seq'), may hold values from -6 to 6
- query_proj: bfloat16 [4, 2048, 512], P('dp', 'seq'), may hold values from -6 to 6
- key_proj: bfloat16 [4, 2048, 128], P('dp', 'seq'), may hold values from -6 to 6
- value_proj: bfloat16 [4, 2048, 128], P('dp', 'seq'), may hold values from -6 to 6
- out_grad: bfloat16 [4, 2048, 512], P('dp', 'seq'), may hold values from -1 to 1
- block_pos: int32 [4, 16], P('dp'), may hold values from 0 to 15, each once within a row
- doc_ids: int32 [4, 16], P('dp'), may hold values from 0 to 7, never falling along the last dimension, each value on 1 to 4 neighbouring positions
Outputs:
- weight_grad: float32 [4096, 768], P(('seq', 'dp'))
The draws below stay inside these ranges and needn't reach their ends.
Inputs may be any that keep to these rules, and one draw needn't show every extreme that they name: Each row is a permutation: storage block j of a sequence holds the tokens of position block block_pos[j] in order. `doc_ids`: along a row the document numbers never fall; each document covers 1 to 4 whole position blocks, and one covers exactly 4.
All inputs are finite; a program needn't handle non-finite values.
Results may differ from the reference program's by a relative error of at most 0.0062.
Values may be sent and summed in bfloat16 or wider, within the bound.
No kernel may reach another device: no remote copies, remote signals or barrier semaphores. Data moves between devices by JAX's collectives and lax.ppermute only.
A program may use at most 64 MiB of HBM per device.

```python
import math
import jax
import jax.numpy as jnp
import numpy as np
from jax import lax

D = 4096
HD = 128
GROUP_Q = 4
BLOCK = 128
QW = 512
QKV = 768
LEN = 2048
BLOCKS = 16
SEQS = 4
DOCS = 8
MOST_DOC = 4


def draw_key_proj(key, part):
    own_key = jax.random.fold_in(key, 17)
    result = jax.random.truncated_normal(own_key, -4.0, 4.0, (SEQS, LEN, HD))
    return result.astype(jnp.bfloat16)


def draw_query_proj(key, part):
    own_key = jax.random.fold_in(key, 29)
    result = jax.random.truncated_normal(own_key, -4.0, 4.0, (SEQS, LEN, GROUP_Q, HD))
    return result.reshape(SEQS, LEN, QW).astype(jnp.bfloat16)


def shard_levels(rng, extent, cuts, low, top_value):
    def one(axis_at, blocks):
        steps = jax.random.uniform(jax.random.fold_in(jax.random.fold_in(rng, 6), axis_at), (blocks,), jnp.float32, low / len(cuts), top_value / len(cuts))
        return jnp.repeat(jnp.exp(steps), extent[axis_at] // blocks).reshape((-1,) + (1,) * (len(extent) - axis_at - 1))

    loudness = one(*cuts[0])
    for cut in cuts[1:]:
        loudness = loudness * one(*cut)
    return loudness


def split_up(count, total, bound, skew):
    weights = [(1 << 20) // math.isqrt(grade ** skew) + 1 for grade in range(2, count + 1)]
    spare, counts = total - bound - (count - 1), [1] * (count - 1)
    while spare > 0:
        free = [i for i in range(count - 1) if counts[i] < bound]
        pool, left = sum([weights[i] for i in free]), spare
        for i in free:
            addition = min(bound - counts[i], max(1, left * weights[i] // pool), spare)
            counts[i] = counts[i] + addition
            spare = spare - addition
    return np.array([bound] + counts)


def ragged(rng, count, total, limit, slope):
    if count == 2:
        one = jax.random.randint(rng, (), max(1, total - limit), min(limit, total - 1) + 1)
        return jnp.stack([one, total - one])
    tallies = jnp.asarray(split_up(count, total, limit, slope), jnp.int32)
    pairs = (count - 1) // 2
    source_of, taker = tallies[1:1 + 2 * pairs:2], tallies[2:2 + 2 * pairs:2]
    margin = jnp.minimum(source_of - 1, limit - taker)
    shifted = jax.random.randint(jax.random.fold_in(rng, 1), (pairs,), 0, 1 << 20) % (margin + 1)
    tallies = tallies.at[1:1 + 2 * pairs:2].set(source_of - shifted).at[2:2 + 2 * pairs:2].set(taker + shifted)
    return tallies[jax.random.permutation(jax.random.fold_in(rng, 2), count)]


def scatter_about(key, dims, scale, most, shards=(), held_as=jnp.bfloat16):
    level = shard_levels(key, dims, shards, -0.22, 0.18) if shards else 1.0
    values = jax.random.normal(key, dims, jnp.float32) * scale * level
    return jnp.minimum(jnp.maximum(values, -most), most).astype(held_as)


def setup_inputs(seed: int = 0) -> dict:
    streams_of = jax.random.split(jax.random.key(seed), 8)
    return {
        "layer_input": scatter_about(streams_of[0], (SEQS, LEN, D), 1.0, 6.0, ((0, 4), (2, 8))),
        "query_proj": draw_query_proj(jax.random.fold_in(streams_of[7], 71), 0),
        "key_proj": draw_key_proj(jax.random.fold_in(streams_of[7], 71), 0),
        "value_proj": scatter_about(streams_of[3], (SEQS, LEN, HD), 1.0, 6.0, ((0, 4), (1, 8))),
        "out_grad": scatter_about(streams_of[4], (SEQS, LEN, QW), (16 * (LEN * SEQS) ** -0.5), 1.0, ((0, 4), (1, 8))),
        "block_pos": jax.vmap(lambda own: jax.random.permutation(own, BLOCKS))(jax.random.split(streams_of[5], SEQS)).reshape((SEQS, BLOCKS)).astype(jnp.int32),
        "doc_ids": jax.vmap(lambda own: jnp.searchsorted(jnp.cumsum(ragged(own, DOCS, BLOCKS, MOST_DOC, 1)), jnp.arange(BLOCKS), side="right"))(jax.random.split(streams_of[6], SEQS)).reshape((SEQS, BLOCKS)).astype(jnp.int32),
    }


def one_sequence(query_s, key_s, value_s, grad_s, pos_row, doc_row):
    precise = lax.Precision.HIGHEST
    row_index = jnp.arange(LEN, dtype=jnp.int32)
    block_at = pos_row[row_index // BLOCK]
    token_pos = block_at * BLOCK + row_index % BLOCK
    token_doc = doc_row[block_at]
    live_mask = (token_doc[:, None] == token_doc[None, :]) & (token_pos[:, None] >= token_pos[None, :])
    scaling = HD ** -0.5
    queries = query_s.astype(jnp.float32).reshape(LEN, GROUP_Q, HD)
    key_rows = key_s.astype(jnp.float32)
    value_rows = value_s.astype(jnp.float32)
    grad_heads = grad_s.astype(jnp.float32).reshape(LEN, GROUP_Q, HD)
    scores = jnp.einsum("ihc,jc->hij", queries, key_rows, precision=precise) * scaling
    masked = jnp.where(live_mask[None], scores, -1e30)
    row_peak = jnp.max(masked, axis=2, keepdims=True)
    weights_exp = jnp.where(live_mask[None], jnp.exp(masked - row_peak), 0.0)
    probs = weights_exp / jnp.sum(weights_exp, axis=2, keepdims=True)
    probs_b = lax.optimization_barrier(probs.astype(jnp.bfloat16)).astype(jnp.float32)
    attended = jnp.einsum("hij,jc->hic", probs_b, value_rows, precision=precise)
    row_delta = jnp.sum(jnp.transpose(grad_heads, (1, 0, 2)) * attended, axis=2)
    dprobs = jnp.einsum("ihc,jc->hij", grad_heads, value_rows, precision=precise)
    dscores = probs * (dprobs - row_delta[..., None])
    dscores = lax.optimization_barrier(dscores.astype(jnp.bfloat16)).astype(jnp.float32)
    query_grad = jnp.einsum("hij,jc->ihc", dscores, key_rows, precision=precise) * scaling
    query_grad = query_grad.reshape(LEN, QW).astype(jnp.bfloat16)
    key_grad = (jnp.einsum("hij,ihc->jc", dscores, queries, precision=precise) * scaling).astype(jnp.bfloat16)
    value_grad = jnp.einsum("hij,ihc->jc", probs_b, grad_heads, precision=precise).astype(jnp.bfloat16)
    return jnp.concatenate([query_grad, key_grad, value_grad], axis=1)


def reference(layer_input, query_proj, key_proj, value_proj, out_grad, block_pos, doc_ids):
    def advance(accum, seq_items):
        input_s, query_s, key_s, value_s, grad_s, pos_row, doc_row = seq_items
        grad_rows = one_sequence(query_s, key_s, value_s, grad_s, pos_row, doc_row)
        weight_term = lax.dot_general(input_s, grad_rows, (((0,), (0,)), ((), ())), preferred_element_type=jnp.float32)
        return accum + weight_term, None

    start_value = jnp.zeros((D, QKV), jnp.float32)
    accum, _ = lax.scan(advance, start_value, (layer_input, query_proj, key_proj, value_proj, out_grad, block_pos, doc_ids))
    return accum
```

```python
import functools

import jax
import jax.numpy as jnp
from jax import lax
from jax.experimental import pallas as pl
from jax.experimental.pallas import tpu as pltpu
from jax.sharding import PartitionSpec as P

masked_fill = -1e30
MOST_DOC = 4
VMEM_LIMIT = 56 * 1024 * 1024

NT = (((1,), (1,)), ((), ()))
NN = (((1,), (0,)), ((), ()))
TN = (((0,), (0,)), ((), ()))


def dot(a, b, dims):
    return lax.dot_general(a, b, dims, preferred_element_type=jnp.float32)


def smem():
    return pl.BlockSpec(memory_space=pltpu.SMEM)


def vmem():
    return pl.BlockSpec(memory_space=pltpu.VMEM)


def kernel_params():
    return pltpu.CompilerParams(vmem_limit_bytes=VMEM_LIMIT)


def attention_kernel(shards, blocks, heads, hd, scaling, *refs):
    me_ref, pos_ref, doc_ref = refs[:3]
    kv_refs = refs[3 : 3 + shards]
    q_refs = refs[3 + shards : 5 + shards]
    g_refs = refs[5 + shards : 7 + shards]
    dq_ref, own_ref = refs[7 + shards : 9 + shards]
    sends = refs[9 + shards : 9 + shards + (shards // 2 - 1)]
    keys, values, dk_acc, dv_acc, inverse = refs[9 + shards + (shards // 2 - 1) :]
    me = me_ref[0]
    per_dev = blocks // shards
    span = keys.shape[0] // blocks

    for rel in range(shards):
        for b in range(per_dev):
            storage = (me ^ rel) * per_dev + b
            place = pos_ref[0, storage]
            inverse[place] = storage
            rows = pl.ds(pl.multiple_of(place * span, span), span)
            keys[rows, :] = kv_refs[rel][b * span : (b + 1) * span, :hd]
            values[rows, :] = kv_refs[rel][b * span : (b + 1) * span, hd:]
    dk_acc[...] = jnp.zeros_like(dk_acc)
    dv_acc[...] = jnp.zeros_like(dv_acc)

    def block_step(which, b, count, first):
        window = pl.ds(pl.multiple_of(first * span, span), count * span)
        key_win = keys[window, :]
        value_win = values[window, :]
        rows = slice(b * span, (b + 1) * span)
        q_cat = jnp.concatenate(
            [q_refs[which][rows, h * hd : (h + 1) * hd] for h in range(heads)], axis=0
        )
        g_cat = jnp.concatenate(
            [g_refs[which][rows, h * hd : (h + 1) * hd] for h in range(heads)], axis=0
        )
        scores = dot(key_win, q_cat, NT)
        dprobs = dot(value_win, g_cat, NT)
        key_at = lax.broadcasted_iota(jnp.int32, (span, heads * span), 0)
        query_at = lax.rem(lax.broadcasted_iota(jnp.int32, (span, heads * span), 1), span)
        last = jnp.where(key_at <= query_at, scores[(count - 1) * span :], masked_fill)
        if count > 1:
            scores = jnp.concatenate([scores[: (count - 1) * span], last], axis=0)
        else:
            scores = last
        peak = jnp.max(scores, axis=0, keepdims=True)
        weights = jnp.exp((scores - peak) * scaling)
        probs = weights * (1.0 / jnp.sum(weights, axis=0, keepdims=True))
        probs_b = probs.astype(jnp.bfloat16)
        delta = jnp.sum(probs_b.astype(jnp.float32) * dprobs, axis=0, keepdims=True)
        dscores = (probs * (dprobs - delta)).astype(jnp.bfloat16)
        dk_new = dot(dscores, q_cat, NN) * scaling
        dv_new = dot(probs_b, g_cat, NN)
        for j in range(count):
            at = pl.ds(pl.multiple_of(inverse[first + j] * span, span), span)
            dk_acc[at, :] += dk_new[j * span : (j + 1) * span]
            dv_acc[at, :] += dv_new[j * span : (j + 1) * span]
        if which == 0:
            dq_new = (dot(dscores, key_win, TN) * scaling).astype(jnp.bfloat16)
            for h in range(heads):
                dq_ref[rows, h * hd : (h + 1) * hd] = dq_new[h * span : (h + 1) * span]

    for which in range(2):
        for b in range(per_dev):
            place = pos_ref[0, (me ^ which) * per_dev + b]
            doc = doc_ref[0, place]
            count = jnp.int32(1)
            for back in range(1, MOST_DOC):
                at = jnp.maximum(place - back, 0)
                same = (place >= back) & (doc_ref[0, at] == doc)
                count = count + same.astype(jnp.int32)
            for n in range(1, MOST_DOC + 1):

                @pl.when(count == n)
                def _():
                    block_step(which, b, n, place - (n - 1))

    tok = per_dev * span

    def shard_rows(rel):
        return pl.ds(pl.multiple_of((me ^ rel) * tok, tok), tok)

    own_ref[:, :hd] = dk_acc[shard_rows(0), :]
    own_ref[:, hd:] = dv_acc[shard_rows(0), :]
    for i, send in enumerate(sends):
        send[:, :hd] = dk_acc[shard_rows(2 * i + 2), :].astype(jnp.bfloat16)
        send[:, hd:] = dv_acc[shard_rows(2 * i + 2), :].astype(jnp.bfloat16)


def attention(me, block_pos, doc_ids, kv_chunks, queries, grads, hd):
    shards = len(kv_chunks)
    tok, qw = queries[0].shape
    blocks = block_pos.shape[1]
    heads = qw // hd
    length = tok * shards
    sends = shards // 2 - 1
    part = jax.ShapeDtypeStruct((tok, 2 * hd), jnp.bfloat16)
    return pl.pallas_call(
        functools.partial(attention_kernel, shards, blocks, heads, hd, hd**-0.5),
        out_shape=(
            jax.ShapeDtypeStruct((tok, qw), jnp.bfloat16),
            jax.ShapeDtypeStruct((tok, 2 * hd), jnp.float32),
        )
        + (part,) * sends,
        in_specs=[smem()] * 3 + [vmem()] * (shards + 4),
        out_specs=(vmem(),) * (2 + sends),
        scratch_shapes=[
            pltpu.VMEM((length, hd), jnp.bfloat16),
            pltpu.VMEM((length, hd), jnp.bfloat16),
            pltpu.VMEM((length, hd), jnp.float32),
            pltpu.VMEM((length, hd), jnp.float32),
            pltpu.SMEM((blocks,), jnp.int32),
        ],
        compiler_params=kernel_params(),
        name="attention",
    )(me, block_pos, doc_ids, *kv_chunks, *queries, *grads)


def sum_kernel(own_ref, *refs):
    total = own_ref[...]
    for ref in refs[:-1]:
        total = total + ref[...].astype(jnp.float32)
    refs[-1][...] = total.astype(refs[-1].dtype)


def sum_parts(own, parts, dtype):
    return pl.pallas_call(
        sum_kernel,
        out_shape=jax.ShapeDtypeStruct(own.shape, dtype),
        in_specs=[vmem()] * (1 + len(parts)),
        out_specs=vmem(),
        compiler_params=kernel_params(),
        name="sum_parts",
    )(own, *parts)


def transpose_kernel(x_ref, out_ref):
    out_ref[...] = x_ref[...].T


def transposed(slab):
    rows, columns = slab.shape
    step = min(rows, 512)
    return pl.pallas_call(
        transpose_kernel,
        grid=(rows // step,),
        out_shape=jax.ShapeDtypeStruct((columns, rows), slab.dtype),
        in_specs=[pl.BlockSpec((step, columns), lambda i: (i, 0))],
        out_specs=pl.BlockSpec((columns, step), lambda i: (0, i)),
        compiler_params=kernel_params(),
        name="slab_transpose",
    )(slab)


def weight_kernel(shards, owners, me_ref, x_ref, *refs):
    chunks = refs[:shards]
    own_ref = refs[shards]
    sends = refs[shards + 1 : shards + owners]
    total = refs[-1]
    me, my_dp = me_ref[0], me_ref[1]
    tok = chunks[0].shape[0]
    for rel in range(shards):
        columns = pl.ds(pl.multiple_of((me ^ rel) * tok, tok), tok)
        term = dot(x_ref[:, columns], chunks[rel][...], NN)
        if rel == 0:
            total[...] = term
        else:
            total[...] += term
    piece = total.shape[0] // owners
    for rel in range(owners):
        rows = pl.ds(pl.multiple_of((my_dp ^ rel) * piece, piece), piece)
        if rel == 0:
            own_ref[...] = total[rows, :]
        else:
            sends[rel - 1][...] = total[rows, :].astype(jnp.bfloat16)


def weight_part(me, x_t, chunks, owners):
    shards = len(chunks)
    features = x_t.shape[0]
    columns = chunks[0].shape[1]
    piece = features // owners
    return pl.pallas_call(
        functools.partial(weight_kernel, shards, owners),
        out_shape=(jax.ShapeDtypeStruct((piece, columns), jnp.float32),)
        + (jax.ShapeDtypeStruct((piece, columns), jnp.bfloat16),) * (owners - 1),
        in_specs=[smem()] + [vmem()] * (1 + shards),
        out_specs=(vmem(),) * owners,
        scratch_shapes=[pltpu.VMEM((features, columns), jnp.float32)],
        compiler_params=kernel_params(),
        name="weight_part",
    )(me, x_t, *chunks)


def final_kernel(groups, owners, *refs):
    out_ref = refs[-1]
    first = 0
    for g in range(groups):
        own = refs[g * owners]
        total = own[...]
        for rel in range(1, owners):
            total = total + refs[g * owners + rel][...].astype(jnp.float32)
        out_ref[:, first : first + own.shape[1]] = total
        first += own.shape[1]


def final_sum(parts):
    groups, owners = len(parts), len(parts[0])
    flat = [array for group in parts for array in group]
    columns = sum(group[0].shape[1] for group in parts)
    return pl.pallas_call(
        functools.partial(final_kernel, groups, owners),
        out_shape=jax.ShapeDtypeStruct((flat[0].shape[0], columns), jnp.float32),
        in_specs=[vmem()] * len(flat),
        out_specs=vmem(),
        compiler_params=kernel_params(),
        name="final_sum",
    )(*flat)


def swap(x, axis, rel):
    return lax.ppermute(x, axis, [(i, i ^ rel) for i in range(lax.axis_size(axis))])


def gather(x):
    shards = lax.axis_size("seq")
    chunks = [None] * shards
    chunks[0] = x
    for rel in range(2, shards, 2):
        chunks[rel] = swap(x, "seq", rel)
    for rel in range(0, shards, 2):
        chunks[rel + 1] = swap(chunks[rel], "seq", 1)
    return chunks


def body(layer_input, query_proj, key_proj, value_proj, out_grad, block_pos, doc_ids):
    shards = lax.axis_size("seq")
    dp = lax.axis_size("dp")
    hd = key_proj.shape[2]
    me = jnp.stack([lax.axis_index("seq"), lax.axis_index("dp")]).astype(jnp.int32)
    kv = jnp.concatenate([key_proj[0], value_proj[0]], axis=1)
    kv_chunks = gather(kv)
    queries = (query_proj[0], swap(query_proj[0], "seq", 1))
    grads = (out_grad[0], swap(out_grad[0], "seq", 1))
    x_t = transposed(layer_input[0])

    dq, own, *sends = attention(me, block_pos, doc_ids, kv_chunks, queries, grads, hd)
    half = dq.shape[1] // 2
    exchanged = [swap(send, "seq", 2 * i + 2) for i, send in enumerate(sends)]
    dkv = sum_parts(own, exchanged, jnp.bfloat16)
    groups = [gather(dq[:, :half]), gather(dq[:, half:]), gather(dkv)]

    if dp <= 8 and dp & (dp - 1) == 0:
        parts = []
        for chunks in groups:
            own_rows, *others = weight_part(me, x_t, chunks, dp)
            parts.append(
                [own_rows] + [swap(other, "dp", i + 1) for i, other in enumerate(others)]
            )
        return final_sum(parts)
    terms = [weight_part(me, x_t, chunks, 1)[0] for chunks in groups]
    return lax.psum_scatter(
        jnp.concatenate(terms, axis=1), "dp", scatter_dimension=0, tiled=True
    )


def solution(mesh):
    placed = (
        P("dp", None, "seq"),
        P("dp", "seq", None),
        P("dp", "seq", None),
        P("dp", "seq", None),
        P("dp", "seq", None),
        P("dp", None),
        P("dp", None),
    )
    return jax.shard_map(
        body, mesh=mesh, in_specs=placed, out_specs=P(("seq", "dp"), None), check_vma=False
    )
```

```python
import functools

import jax
import jax.numpy as jnp
from jax import lax
from jax.experimental import pallas as pl
from jax.experimental.pallas import tpu as pltpu
from jax.sharding import PartitionSpec as P

masked_fill = -1e30
MOST_DOC = 4
VMEM_LIMIT = 20 * 1024 * 1024

NT = (((1,), (1,)), ((), ()))
NN = (((1,), (0,)), ((), ()))
TN = (((0,), (0,)), ((), ()))


def dot(a, b, dims):
    return lax.dot_general(a, b, dims, preferred_element_type=jnp.float32)


def smem():
    return pl.BlockSpec(memory_space=pltpu.SMEM)


def vmem():
    return pl.BlockSpec(memory_space=pltpu.VMEM)


def kernel_params():
    return pltpu.CompilerParams(vmem_limit_bytes=VMEM_LIMIT)


def attention_kernel(shards, blocks, heads, hd, scaling, *refs):
    me_ref, pos_ref, doc_ref = refs[:3]
    kv_refs = refs[3 : 3 + shards]
    q_refs = refs[3 + shards : 5 + shards]
    g_refs = refs[5 + shards : 7 + shards]
    dq_ref, own_ref = refs[7 + shards : 9 + shards]
    sends = refs[9 + shards : 9 + shards + (shards // 2 - 1)]
    keys, values, dk_acc, dv_acc, inverse = refs[9 + shards + (shards // 2 - 1) :]
    me = me_ref[0]
    per_dev = blocks // shards
    span = keys.shape[0] // blocks

    for rel in range(shards):
        for b in range(per_dev):
            storage = (me ^ rel) * per_dev + b
            place = pos_ref[0, storage]
            inverse[place] = storage
            rows = pl.ds(pl.multiple_of(place * span, span), span)
            keys[rows, :] = kv_refs[rel][b * span : (b + 1) * span, :hd]
            values[rows, :] = kv_refs[rel][b * span : (b + 1) * span, hd:]
    dk_acc[...] = jnp.zeros_like(dk_acc)
    dv_acc[...] = jnp.zeros_like(dv_acc)

    def block_step(which, b, count, first):
        window = pl.ds(pl.multiple_of(first * span, span), count * span)
        key_win = keys[window, :]
        value_win = values[window, :]
        rows = slice(b * span, (b + 1) * span)
        q_cat = jnp.concatenate(
            [q_refs[which][rows, h * hd : (h + 1) * hd] for h in range(heads)], axis=0
        )
        g_cat = jnp.concatenate(
            [g_refs[which][rows, h * hd : (h + 1) * hd] for h in range(heads)], axis=0
        )
        scores = dot(key_win, q_cat, NT)
        dprobs = dot(value_win, g_cat, NT)
        key_at = lax.broadcasted_iota(jnp.int32, (span, heads * span), 0)
        query_at = lax.rem(lax.broadcasted_iota(jnp.int32, (span, heads * span), 1), span)
        last = jnp.where(key_at <= query_at, scores[(count - 1) * span :], masked_fill)
        if count > 1:
            scores = jnp.concatenate([scores[: (count - 1) * span], last], axis=0)
        else:
            scores = last
        peak = jnp.max(scores, axis=0, keepdims=True)
        weights = jnp.exp((scores - peak) * scaling)
        probs = weights * (1.0 / jnp.sum(weights, axis=0, keepdims=True))
        probs_b = probs.astype(jnp.bfloat16)
        delta = jnp.sum(probs_b.astype(jnp.float32) * dprobs, axis=0, keepdims=True)
        dscores = (probs * (dprobs - delta)).astype(jnp.bfloat16)
        dk_new = dot(dscores, q_cat, NN) * scaling
        dv_new = dot(probs_b, g_cat, NN)
        for j in range(count):
            at = pl.ds(pl.multiple_of(inverse[first + j] * span, span), span)
            dk_acc[at, :] += dk_new[j * span : (j + 1) * span]
            dv_acc[at, :] += dv_new[j * span : (j + 1) * span]
        if which == 0:
            dq_new = (dot(dscores, key_win, TN) * scaling).astype(jnp.bfloat16)
            for h in range(heads):
                dq_ref[rows, h * hd : (h + 1) * hd] = dq_new[h * span : (h + 1) * span]

    for which in range(2):
        for b in range(per_dev):
            place = pos_ref[0, (me ^ which) * per_dev + b]
            doc = doc_ref[0, place]
            count = jnp.int32(1)
            for back in range(1, MOST_DOC):
                at = jnp.maximum(place - back, 0)
                same = (place >= back) & (doc_ref[0, at] == doc)
                count = count + same.astype(jnp.int32)
            for n in range(1, MOST_DOC + 1):

                @pl.when(count == n)
                def _():
                    block_step(which, b, n, place - (n - 1))

    tok = per_dev * span

    def shard_rows(rel):
        return pl.ds(pl.multiple_of((me ^ rel) * tok, tok), tok)

    own_ref[:, :hd] = dk_acc[shard_rows(0), :]
    own_ref[:, hd:] = dv_acc[shard_rows(0), :]
    for i, send in enumerate(sends):
        send[:, :hd] = dk_acc[shard_rows(2 * i + 2), :].astype(jnp.bfloat16)
        send[:, hd:] = dv_acc[shard_rows(2 * i + 2), :].astype(jnp.bfloat16)


def attention(me, block_pos, doc_ids, kv_chunks, queries, grads, hd):
    shards = len(kv_chunks)
    tok, qw = queries[0].shape
    blocks = block_pos.shape[1]
    heads = qw // hd
    length = tok * shards
    sends = shards // 2 - 1
    part = jax.ShapeDtypeStruct((tok, 2 * hd), jnp.bfloat16)
    return pl.pallas_call(
        functools.partial(attention_kernel, shards, blocks, heads, hd, hd**-0.5),
        out_shape=(
            jax.ShapeDtypeStruct((tok, qw), jnp.bfloat16),
            jax.ShapeDtypeStruct((tok, 2 * hd), jnp.float32),
        )
        + (part,) * sends,
        in_specs=[smem()] * 3 + [vmem()] * (shards + 4),
        out_specs=(vmem(),) * (2 + sends),
        scratch_shapes=[
            pltpu.VMEM((length, hd), jnp.bfloat16),
            pltpu.VMEM((length, hd), jnp.bfloat16),
            pltpu.VMEM((length, hd), jnp.float32),
            pltpu.VMEM((length, hd), jnp.float32),
            pltpu.SMEM((blocks,), jnp.int32),
        ],
        compiler_params=kernel_params(),
        name="attention",
    )(me, block_pos, doc_ids, *kv_chunks, *queries, *grads)


def sum_kernel(own_ref, *refs):
    total = own_ref[...]
    for ref in refs[:-1]:
        total = total + ref[...].astype(jnp.float32)
    refs[-1][...] = total.astype(refs[-1].dtype)


def sum_parts(own, parts, dtype):
    return pl.pallas_call(
        sum_kernel,
        out_shape=jax.ShapeDtypeStruct(own.shape, dtype),
        in_specs=[vmem()] * (1 + len(parts)),
        out_specs=vmem(),
        compiler_params=kernel_params(),
        name="sum_parts",
    )(own, *parts)


def weight_kernel(shards, owners, me_ref, x_ref, *refs):
    chunks = refs[:shards]
    own_ref = refs[shards]
    sends = refs[shards + 1 : shards + owners]
    rows_all, total = refs[-2:]
    me, my_dp = me_ref[0], me_ref[1]
    tok = chunks[0].shape[0]
    for rel in range(shards):
        rows_all[pl.ds(pl.multiple_of((me ^ rel) * tok, tok), tok), :] = chunks[rel][...]
    total[...] = dot(x_ref[...], rows_all[...], TN)
    piece = total.shape[0] // owners
    for rel in range(owners):
        rows = pl.ds(pl.multiple_of((my_dp ^ rel) * piece, piece), piece)
        if rel == 0:
            own_ref[...] = total[rows, :]
        else:
            sends[rel - 1][...] = total[rows, :].astype(jnp.bfloat16)


def weight_part(me, slab, chunks, owners):
    shards = len(chunks)
    length, features = slab.shape
    columns = chunks[0].shape[1]
    piece = features // owners
    return pl.pallas_call(
        functools.partial(weight_kernel, shards, owners),
        out_shape=(jax.ShapeDtypeStruct((piece, columns), jnp.float32),)
        + (jax.ShapeDtypeStruct((piece, columns), jnp.bfloat16),) * (owners - 1),
        in_specs=[smem()] + [vmem()] * (1 + shards),
        out_specs=(vmem(),) * owners,
        scratch_shapes=[
            pltpu.VMEM((length, columns), jnp.bfloat16),
            pltpu.VMEM((features, columns), jnp.float32),
        ],
        compiler_params=kernel_params(),
        cost_estimate=pl.CostEstimate(
            flops=2 * length * features * columns,
            bytes_accessed=2 * length * (features + columns),
            transcendentals=0,
        ),
        name="weight_part",
    )(me, slab, *chunks)


def final_kernel(groups, owners, *refs):
    out_ref = refs[-1]
    first = 0
    for g in range(groups):
        own = refs[g * owners]
        total = own[...]
        for rel in range(1, owners):
            total = total + refs[g * owners + rel][...].astype(jnp.float32)
        out_ref[:, first : first + own.shape[1]] = total
        first += own.shape[1]


def final_sum(parts):
    groups, owners = len(parts), len(parts[0])
    flat = [array for group in parts for array in group]
    columns = sum(group[0].shape[1] for group in parts)
    return pl.pallas_call(
        functools.partial(final_kernel, groups, owners),
        out_shape=jax.ShapeDtypeStruct((flat[0].shape[0], columns), jnp.float32),
        in_specs=[vmem()] * len(flat),
        out_specs=vmem(),
        compiler_params=kernel_params(),
        name="final_sum",
    )(*flat)


def swap(x, axis, rel):
    return lax.ppermute(x, axis, [(i, i ^ rel) for i in range(lax.axis_size(axis))])


def gather(x):
    shards = lax.axis_size("seq")
    chunks = [None] * shards
    chunks[0] = x
    for rel in range(2, shards, 2):
        chunks[rel] = swap(x, "seq", rel)
    for rel in range(0, shards, 2):
        chunks[rel + 1] = swap(chunks[rel], "seq", 1)
    return chunks


def body(layer_input, query_proj, key_proj, value_proj, out_grad, block_pos, doc_ids):
    shards = lax.axis_size("seq")
    dp = lax.axis_size("dp")
    hd = key_proj.shape[2]
    me = jnp.stack([lax.axis_index("seq"), lax.axis_index("dp")]).astype(jnp.int32)
    kv = jnp.concatenate([key_proj[0], value_proj[0]], axis=1)
    kv_chunks = gather(kv)
    queries = (query_proj[0], swap(query_proj[0], "seq", 1))
    grads = (out_grad[0], swap(out_grad[0], "seq", 1))
    slab = layer_input[0]
    dq, own, *sends = attention(me, block_pos, doc_ids, kv_chunks, queries, grads, hd)
    half = dq.shape[1] // 2
    exchanged = [swap(send, "seq", 2 * i + 2) for i, send in enumerate(sends)]
    dkv = sum_parts(own, exchanged, jnp.bfloat16)
    groups = [gather(dq[:, :half]), gather(dq[:, half:]), gather(dkv)]

    if dp <= 8 and dp & (dp - 1) == 0:
        parts = []
        for chunks in groups:
            own_rows, *others = weight_part(me, slab, chunks, dp)
            parts.append(
                [own_rows] + [swap(other, "dp", i + 1) for i, other in enumerate(others)]
            )
        return final_sum(parts)
    terms = [weight_part(me, slab, chunks, 1)[0] for chunks in groups]
    return lax.psum_scatter(
        jnp.concatenate(terms, axis=1), "dp", scatter_dimension=0, tiled=True
    )


def solution(mesh):
    placed = (
        P("dp", None, "seq"),
        P("dp", "seq", None),
        P("dp", "seq", None),
        P("dp", "seq", None),
        P("dp", "seq", None),
        P("dp", None),
        P("dp", None),
    )
    return jax.shard_map(
        body, mesh=mesh, in_specs=placed, out_specs=P(("seq", "dp"), None), check_vma=False
    )
```

```python
import functools
import math

import jax
import jax.numpy as jnp
from jax import lax
from jax.experimental import pallas as pl
from jax.experimental.pallas import tpu as pltpu
from jax.sharding import PartitionSpec as P

masked_fill = -1e30
MOST_DOC = 4
TOGETHER = 2
AT_ONCE = {1: (4, 2, 1), 2: (2, 1), 3: (1,), 4: (1,)}
VMEM_LIMIT = 24 * 1024 * 1024

NT = (((1,), (1,)), ((), ()))
NN = (((1,), (0,)), ((), ()))
TN = (((0,), (0,)), ((), ()))


def dot(a, b, dims):
    return lax.dot_general(a, b, dims, preferred_element_type=jnp.float32)


def smem():
    return pl.BlockSpec(memory_space=pltpu.SMEM)


def vmem():
    return pl.BlockSpec(memory_space=pltpu.VMEM)


def kernel_params():
    return pltpu.CompilerParams(vmem_limit_bytes=VMEM_LIMIT)


def swap(x, axis, rel):
    return lax.ppermute(x, axis, [(i, i ^ rel) for i in range(lax.axis_size(axis))])


def routes(shards):
    bits = [1 << b for b in range(1, shards.bit_length() - 1)]
    return bits, bits[::-1]


def across(x, step):
    shards = lax.axis_size("seq")
    even, odd = routes(shards)
    pairs = [(i, i ^ (odd if i & 1 else even)[step]) for i in range(shards)]
    return lax.ppermute(x, "seq", pairs)


def from_chips(x):
    chunks = [x]
    for step in range(len(routes(lax.axis_size("seq"))[0])):
        chunks += [across(chunk, step) for chunk in chunks]
    return chunks


def with_other_core(chunks):
    return [part for chunk in chunks for part in (chunk, swap(chunk, "seq", 1))]


def origin(me, place, shards):
    def offset(order):
        return sum(bit for j, bit in enumerate(order) if (place >> 1) >> j & 1)

    even, odd = (offset(order) for order in routes(shards))
    core = me & 1
    if place & 1:
        return me ^ 1 ^ (odd + (even - odd) * core)
    return me ^ (even + (odd - even) * core)


def attention_kernel(shards, blocks, heads, hd, kv_at, q_at, scaling, last, *refs):
    meta = refs[0]
    kv_refs = refs[1 : 1 + shards]
    q_refs = refs[1 + shards : 1 + 2 * shards]
    refs = refs[1 + 2 * shards :]
    if last:
        dk_before, dv_before, dq_ref, dk_ref, dv_ref = refs[:5]
        refs = refs[5:]
    else:
        dq_ref, dk_ref, dv_ref = refs[:3]
        refs = refs[3:]
    keys, values, queries, grads, inverse, starts = refs
    me = meta[0]
    per_dev = blocks // shards
    span = keys.shape[0] // blocks
    qw = heads * hd

    def document(place):
        return meta[2 + blocks + place]

    def rows_at(first, count):
        return pl.ds(pl.multiple_of(first * span, span), count * span)

    for place in range(shards):
        device = origin(me, place, shards)
        for b in range(per_dev):
            storage = device * per_dev + b
            position = meta[2 + storage]
            inverse[position] = storage
            rows = rows_at(position, 1)
            here = slice(b * span, (b + 1) * span)
            keys[rows, :] = kv_refs[place][here, kv_at : kv_at + hd]
            values[rows, :] = kv_refs[place][here, kv_at + hd : kv_at + 2 * hd]
            queries[rows, :] = q_refs[place][here, q_at : q_at + qw]
            grads[rows, :] = q_refs[place][here, q_at + qw : q_at + 2 * qw]

    def note(state):
        first, counts = state[0], state[1:]
        size = jnp.int32(1)
        for ahead in range(1, MOST_DOC):
            at = jnp.minimum(first + ahead, blocks - 1)
            same = (first + ahead < blocks) & (document(at) == document(first))
            size = size + same.astype(jnp.int32)
        listed = counts[0]
        for n in range(2, MOST_DOC + 1):
            listed = jnp.where(size == n, counts[n - 1], listed)
        starts[(size - 1) * blocks + listed] = first
        counts = tuple(
            count + (size == n + 1).astype(jnp.int32) for n, count in enumerate(counts)
        )
        return (first + size,) + counts

    listed = lax.while_loop(
        lambda state: state[0] < blocks, note, (jnp.int32(0),) * (MOST_DOC + 1)
    )[1:]

    def stacked(ref, first, count):
        return jnp.concatenate(
            [ref[rows_at(first, count), h * hd : (h + 1) * hd] for h in range(heads)], axis=0
        )

    def masked(scores, before, count):
        square = (count * span, heads * count * span)
        key_at = lax.broadcasted_iota(jnp.int32, square, 0)
        query_at = lax.rem(lax.broadcasted_iota(jnp.int32, square, 1), count * span)
        diagonal = jnp.where(key_at <= query_at, scores[before * span :], masked_fill)
        if not before:
            return diagonal
        return jnp.concatenate([scores[: before * span], diagonal], axis=0)

    def step(firsts, size):
        parts = [
            (first, before, min(TOGETHER, size - before))
            for first in firsts
            for before in range(0, size, TOGETHER)
        ]
        q_cats = [stacked(queries, first + before, count) for first, before, count in parts]
        g_cats = [stacked(grads, first + before, count) for first, before, count in parts]
        key_wins = [keys[rows_at(first, before + count), :] for first, before, count in parts]
        value_wins = [values[rows_at(first, before + count), :] for first, before, count in parts]
        scores = [dot(key_win, q_cat, NT) for key_win, q_cat in zip(key_wins, q_cats)]
        dprobs = [dot(value_win, g_cat, NT) for value_win, g_cat in zip(value_wins, g_cats)]
        scores = [masked(s, before, count) for s, (_, before, count) in zip(scores, parts)]
        peaks = [jnp.max(s, axis=0, keepdims=True) for s in scores]
        weights = [
            jnp.exp2((s - peak) * (scaling * math.log2(math.e)))
            for s, peak in zip(scores, peaks)
        ]
        shares = [1.0 / jnp.sum(w, axis=0, keepdims=True) for w in weights]
        probs = [w * share for w, share in zip(weights, shares)]
        probs_b = [p.astype(jnp.bfloat16) for p in probs]
        deltas = [
            jnp.sum(p.astype(jnp.float32) * dp, axis=0, keepdims=True)
            for p, dp in zip(probs_b, dprobs)
        ]
        dscores = [
            (p * (dp - delta)).astype(jnp.bfloat16)
            for p, dp, delta in zip(probs, dprobs, deltas)
        ]
        dks = [dot(ds, q_cat, NN) for ds, q_cat in zip(dscores, q_cats)]
        dvs = [dot(p, g_cat, NN) for p, g_cat in zip(probs_b, g_cats)]
        dqs = [
            (dot(ds, key_win, TN) * scaling).astype(jnp.bfloat16)
            for ds, key_win in zip(dscores, key_wins)
        ]
        for dq, (first, before, count) in zip(dqs, parts):
            for t in range(count):
                at = rows_at(inverse[first + before + t], 1)
                for h in range(heads):
                    start = (h * count + t) * span
                    dq_ref[at, h * hd : (h + 1) * hd] = dq[start : start + span]
        for first in firsts:
            for j in range(size):
                reach = [
                    i
                    for i, (start, before, count) in enumerate(parts)
                    if start is first and before + count > j
                ]
                rows = slice(j * span, (j + 1) * span)
                dk = sum(dks[i][rows] for i in reach) * scaling
                dv = sum(dvs[i][rows] for i in reach)
                at = rows_at(inverse[first + j], 1)
                if last:
                    dk, dv = dk + dk_before[at, :], dv + dv_before[at, :]
                dk_ref[at, :] = dk.astype(dk_ref.dtype)
                dv_ref[at, :] = dv.astype(dv_ref.dtype)

    for size in range(MOST_DOC, 0, -1):
        done = jnp.int32(0)
        for together in AT_ONCE[size]:
            times = (listed[size - 1] - done) // together

            def some(k, carry, size=size, together=together, done=done):
                at = (size - 1) * blocks + done + k * together
                step([starts[at + d] for d in range(together)], size)
                return carry

            lax.fori_loop(0, times, some, jnp.int32(0))
            done = done + times * together


def attention(meta, blocks, hd, heads, kv_chunks, kv_at, q_chunks, q_at, before, last):
    shards = len(kv_chunks)
    length = kv_chunks[0].shape[0] * shards
    qw = heads * hd
    sums = jnp.bfloat16 if last else jnp.float32
    return pl.pallas_call(
        functools.partial(
            attention_kernel, shards, blocks, heads, hd, kv_at, q_at, hd**-0.5, last
        ),
        out_shape=(
            jax.ShapeDtypeStruct((length, qw), jnp.bfloat16),
            jax.ShapeDtypeStruct((length, hd), sums),
            jax.ShapeDtypeStruct((length, hd), sums),
        ),
        in_specs=[smem()] + [vmem()] * (2 * shards + len(before)),
        out_specs=(vmem(),) * 3,
        scratch_shapes=[
            pltpu.VMEM((length, hd), jnp.bfloat16),
            pltpu.VMEM((length, hd), jnp.bfloat16),
            pltpu.VMEM((length, qw), jnp.bfloat16),
            pltpu.VMEM((length, qw), jnp.bfloat16),
            pltpu.SMEM((blocks,), jnp.int32),
            pltpu.SMEM((MOST_DOC * blocks,), jnp.int32),
        ],
        compiler_params=kernel_params(),
        cost_estimate=pl.CostEstimate(
            flops=10 * 2 * length * span_of(length, blocks) * qw,
            bytes_accessed=24 * length * qw,
            transcendentals=2 * length * span_of(length, blocks) * heads,
        ),
        name="attention",
    )(meta, *kv_chunks, *q_chunks, *before)


def span_of(length, blocks):
    return length // blocks


def weight_kernel(owners, parts, meta, slab_ref, *refs):
    rows_refs = refs[:parts]
    own_ref = refs[parts]
    sends = refs[parts + 1 : parts + owners]
    total = refs[-1]
    my_dp = meta[1]
    first = 0
    for ref in rows_refs:
        width = ref.shape[1]
        total[:, first : first + width] = dot(slab_ref[...], ref[...], TN)
        first += width
    piece = total.shape[0] // owners
    for rel in range(owners):
        rows = pl.ds(pl.multiple_of((my_dp ^ rel) * piece, piece), piece)
        if rel == 0:
            own_ref[...] = total[rows, :]
        else:
            sends[rel - 1][...] = total[rows, :].astype(jnp.bfloat16)


def weight_part(meta, slab, grads, owners):
    length, features = slab.shape
    columns = sum(part.shape[1] for part in grads)
    piece = features // owners
    return pl.pallas_call(
        functools.partial(weight_kernel, owners, len(grads)),
        out_shape=(jax.ShapeDtypeStruct((piece, columns), jnp.float32),)
        + (jax.ShapeDtypeStruct((piece, columns), jnp.bfloat16),) * (owners - 1),
        in_specs=[smem()] + [vmem()] * (1 + len(grads)),
        out_specs=(vmem(),) * owners,
        scratch_shapes=[pltpu.VMEM((features, columns), jnp.float32)],
        compiler_params=kernel_params(),
        cost_estimate=pl.CostEstimate(
            flops=2 * length * features * columns,
            bytes_accessed=2 * length * (features + columns),
            transcendentals=0,
        ),
        name="weight_part",
    )(meta, slab, *grads)


def final_kernel(groups, owners, *refs):
    out_ref = refs[-1]
    first = 0
    for g in range(groups):
        own = refs[g * owners]
        total = own[...]
        for rel in range(1, owners):
            total = total + refs[g * owners + rel][...].astype(jnp.float32)
        for columns, width in out_columns(g, groups, own.shape[1], out_ref.shape[1]):
            out_ref[:, columns : columns + width] = total[:, first : first + width]
            first += width
        first = 0


def out_columns(group, groups, width, whole):
    return [(0, width)] if group == 0 else [(whole - width, width)]


def final_sum(parts):
    groups, owners = len(parts), len(parts[0])
    flat = [array for group in parts for array in group]
    columns = sum(group[0].shape[1] for group in parts)
    return pl.pallas_call(
        functools.partial(final_kernel, groups, owners),
        out_shape=jax.ShapeDtypeStruct((flat[0].shape[0], columns), jnp.float32),
        in_specs=[vmem()] * len(flat),
        out_specs=vmem(),
        compiler_params=kernel_params(),
        name="final_sum",
    )(*flat)


def ordered(first, later):
    return lax.optimization_barrier((first, later))


def body(layer_input, query_proj, key_proj, value_proj, out_grad, block_pos, doc_ids):
    dp = lax.axis_size("dp")
    blocks = block_pos.shape[1]
    hd = key_proj.shape[2]
    qw = query_proj.shape[2]
    half = qw // 2
    heads = half // hd
    me = jnp.stack([lax.axis_index("seq"), lax.axis_index("dp")]).astype(jnp.int32)
    meta = jnp.concatenate([me, block_pos[0], doc_ids[0]])
    slab = layer_input[0]

    first = jnp.concatenate(
        [key_proj[0], value_proj[0], query_proj[0, :, :half], out_grad[0, :, :half]], axis=1
    )
    first_sent = [across(first, step) for step in range(2)]
    first_sent[0], (queries, grads, meta) = ordered(
        first_sent[0], (query_proj[0], out_grad[0], meta)
    )
    first_sent.append(across(first_sent[0], 1))
    second = jnp.concatenate([queries[:, half:], grads[:, half:]], axis=1)
    second_sent = [across(second, step) for step in range(2)]
    first_sent, second_sent = ordered(first_sent, second_sent)
    second_sent.append(across(second_sent[0], 1))
    first_chunks = with_other_core([first] + first_sent)

    exchange = dp <= 8 and dp & (dp - 1) == 0
    owners = dp if exchange else 1

    def over_dp(terms):
        return [terms[0]] + [swap(term, "dp", i + 1) for i, term in enumerate(terms[1:])]

    early, *sums = attention(
        meta, blocks, hd, heads, first_chunks, 0, first_chunks, 2 * hd, [], False
    )
    second_sent, early = ordered(second_sent, early)
    second_chunks = with_other_core([second] + second_sent)
    early_terms = over_dp(weight_part(meta, slab, [early], owners))
    late, dk, dv = attention(
        meta, blocks, hd, heads, first_chunks, 0, second_chunks, 0, sums, True
    )
    early_terms, late = ordered(early_terms, late)
    late_terms = over_dp(weight_part(meta, slab, [late, dk, dv], owners))
    groups = (early_terms, late_terms)
    if exchange:
        return final_sum(groups)
    return lax.psum_scatter(
        jnp.concatenate([terms[0] for terms in groups], axis=1),
        "dp",
        scatter_dimension=0,
        tiled=True,
    )


def solution(mesh):
    placed = (
        P("dp", None, "seq"),
        P("dp", "seq", None),
        P("dp", "seq", None),
        P("dp", "seq", None),
        P("dp", "seq", None),
        P("dp", None),
        P("dp", None),
    )
    return jax.shard_map(
        body, mesh=mesh, in_specs=placed, out_specs=P(("seq", "dp"), None), check_vma=False
    )
```

```python
import functools
import math

import jax
import jax.numpy as jnp
from jax import lax
from jax.experimental import pallas as pl
from jax.experimental.pallas import tpu as pltpu
from jax.sharding import PartitionSpec as P

masked_fill = -1e30
MOST_DOC = 4
TOGETHER = 1
AT_ONCE = {1: (4, 2, 1), 2: (2, 1), 3: (1,), 4: (1,)}
VMEM_LIMIT = 24 * 1024 * 1024

NT = (((1,), (1,)), ((), ()))
NN = (((1,), (0,)), ((), ()))
TN = (((0,), (0,)), ((), ()))


def dot(a, b, dims):
    return lax.dot_general(a, b, dims, preferred_element_type=jnp.float32)


def smem():
    return pl.BlockSpec(memory_space=pltpu.SMEM)


def vmem():
    return pl.BlockSpec(memory_space=pltpu.VMEM)


def kernel_params():
    return pltpu.CompilerParams(vmem_limit_bytes=VMEM_LIMIT)


def swap(x, axis, rel):
    return lax.ppermute(x, axis, [(i, i ^ rel) for i in range(lax.axis_size(axis))])


def routes(shards):
    bits = [1 << b for b in range(1, shards.bit_length() - 1)]
    return bits, bits[::-1]


def across(x, step):
    shards = lax.axis_size("seq")
    even, odd = routes(shards)
    pairs = [(i, i ^ (odd if i & 1 else even)[step]) for i in range(shards)]
    return lax.ppermute(x, "seq", pairs)


def from_chips(x):
    chunks = [x]
    for step in range(len(routes(lax.axis_size("seq"))[0])):
        chunks += [across(chunk, step) for chunk in chunks]
    return chunks


def with_other_core(chunks):
    return [part for chunk in chunks for part in (chunk, swap(chunk, "seq", 1))]


def origin(me, place, shards):
    def offset(order):
        return sum(bit for j, bit in enumerate(order) if (place >> 1) >> j & 1)

    even, odd = (offset(order) for order in routes(shards))
    core = me & 1
    if place & 1:
        return me ^ 1 ^ (odd + (even - odd) * core)
    return me ^ (even + (odd - even) * core)


def attention_kernel(shards, blocks, heads, hd, scaling, *refs):
    meta = refs[0]
    chunks = refs[1 : 1 + shards]
    dq_refs = refs[1 + shards : -8]
    dk_ref, dv_ref, keys, values, queries, grads, inverse, starts = refs[-8:]
    me = meta[0]
    per_dev = blocks // shards
    span = keys.shape[0] // blocks
    qw = heads * hd

    def document(place):
        return meta[2 + blocks + place]

    def rows_at(first, count):
        return pl.ds(pl.multiple_of(first * span, span), count * span)

    for place in range(shards):
        device = origin(me, place, shards)
        for b in range(per_dev):
            storage = device * per_dev + b
            position = meta[2 + storage]
            inverse[position] = storage
            rows = rows_at(position, 1)
            here = slice(b * span, (b + 1) * span)
            at = 0
            for whole in (keys, values, queries, grads):
                whole[rows, :] = chunks[place][here, at : at + whole.shape[1]]
                at += whole.shape[1]

    def note(state):
        first, counts = state[0], state[1:]
        size = jnp.int32(1)
        for ahead in range(1, MOST_DOC):
            at = jnp.minimum(first + ahead, blocks - 1)
            same = (first + ahead < blocks) & (document(at) == document(first))
            size = size + same.astype(jnp.int32)
        listed = counts[0]
        for n in range(2, MOST_DOC + 1):
            listed = jnp.where(size == n, counts[n - 1], listed)
        starts[(size - 1) * blocks + listed] = first
        counts = tuple(
            count + (size == n + 1).astype(jnp.int32) for n, count in enumerate(counts)
        )
        return (first + size,) + counts

    listed = lax.while_loop(
        lambda state: state[0] < blocks, note, (jnp.int32(0),) * (MOST_DOC + 1)
    )[1:]

    def stacked(ref, first, count):
        return jnp.concatenate(
            [ref[rows_at(first, count), h * hd : (h + 1) * hd] for h in range(heads)], axis=0
        )

    def masked(scores, before, count):
        square = (count * span, heads * count * span)
        key_at = lax.broadcasted_iota(jnp.int32, square, 0)
        query_at = lax.rem(lax.broadcasted_iota(jnp.int32, square, 1), count * span)
        diagonal = jnp.where(key_at <= query_at, scores[before * span :], masked_fill)
        if not before:
            return diagonal
        return jnp.concatenate([scores[: before * span], diagonal], axis=0)

    def step(firsts, size):
        parts = [
            (first, before, min(TOGETHER, size - before))
            for first in firsts
            for before in range(0, size, TOGETHER)
        ]
        q_cats = [stacked(queries, first + before, count) for first, before, count in parts]
        g_cats = [stacked(grads, first + before, count) for first, before, count in parts]
        key_wins = [keys[rows_at(first, before + count), :] for first, before, count in parts]
        value_wins = [values[rows_at(first, before + count), :] for first, before, count in parts]
        scores = [dot(key_win, q_cat, NT) for key_win, q_cat in zip(key_wins, q_cats)]
        dprobs = [dot(value_win, g_cat, NT) for value_win, g_cat in zip(value_wins, g_cats)]
        scores = [masked(s, before, count) for s, (_, before, count) in zip(scores, parts)]
        peaks = [jnp.max(s, axis=0, keepdims=True) for s in scores]
        weights = [
            jnp.exp2((s - peak) * (scaling * math.log2(math.e)))
            for s, peak in zip(scores, peaks)
        ]
        shares = [1.0 / jnp.sum(w, axis=0, keepdims=True) for w in weights]
        probs = [w * share for w, share in zip(weights, shares)]
        probs_b = [p.astype(jnp.bfloat16) for p in probs]
        deltas = [
            jnp.sum(p.astype(jnp.float32) * dp, axis=0, keepdims=True)
            for p, dp in zip(probs_b, dprobs)
        ]
        dscores = [
            (p * (dp - delta)).astype(jnp.bfloat16)
            for p, dp, delta in zip(probs, dprobs, deltas)
        ]
        dks = [dot(ds, q_cat, NN) for ds, q_cat in zip(dscores, q_cats)]
        dvs = [dot(p, g_cat, NN) for p, g_cat in zip(probs_b, g_cats)]
        dqs = [
            (dot(ds, key_win, TN) * scaling).astype(jnp.bfloat16)
            for ds, key_win in zip(dscores, key_wins)
        ]
        for dq, (first, before, count) in zip(dqs, parts):
            for t in range(count):
                at = rows_at(inverse[first + before + t], 1)
                for h in range(heads):
                    start = (h * count + t) * span
                    dq_ref = dq_refs[h * len(dq_refs) // heads]
                    column = h * hd % dq_ref.shape[1]
                    dq_ref[at, column : column + hd] = dq[start : start + span]
        for first in firsts:
            for j in range(size):
                reach = [
                    i
                    for i, (start, before, count) in enumerate(parts)
                    if start is first and before + count > j
                ]
                rows = slice(j * span, (j + 1) * span)
                dk = sum(dks[i][rows] for i in reach) * scaling
                dv = sum(dvs[i][rows] for i in reach)
                at = rows_at(inverse[first + j], 1)
                dk_ref[at, :] = dk.astype(dk_ref.dtype)
                dv_ref[at, :] = dv.astype(dv_ref.dtype)

    for size in range(MOST_DOC, 0, -1):
        done = jnp.int32(0)
        for together in AT_ONCE[size]:
            times = (listed[size - 1] - done) // together

            def some(k, carry, size=size, together=together, done=done):
                at = (size - 1) * blocks + done + k * together
                step([starts[at + d] for d in range(together)], size)
                return carry

            lax.fori_loop(0, times, some, jnp.int32(0))
            done = done + times * together


def attention(meta, blocks, hd, chunks, groups):
    shards = len(chunks)
    tok, columns = chunks[0].shape
    length = tok * shards
    qw = (columns - 2 * hd) // 2
    outs = (qw // groups,) * groups + (hd, hd)
    pairs = length * length // blocks
    return pl.pallas_call(
        functools.partial(attention_kernel, shards, blocks, qw // hd, hd, hd**-0.5),
        out_shape=tuple(jax.ShapeDtypeStruct((length, width), jnp.bfloat16) for width in outs),
        in_specs=[smem()] + [vmem()] * shards,
        out_specs=(vmem(),) * len(outs),
        scratch_shapes=[
            pltpu.VMEM((length, hd), jnp.bfloat16),
            pltpu.VMEM((length, hd), jnp.bfloat16),
            pltpu.VMEM((length, qw), jnp.bfloat16),
            pltpu.VMEM((length, qw), jnp.bfloat16),
            pltpu.SMEM((blocks,), jnp.int32),
            pltpu.SMEM((MOST_DOC * blocks,), jnp.int32),
        ],
        compiler_params=kernel_params(),
        cost_estimate=pl.CostEstimate(
            flops=20 * pairs * qw,
            bytes_accessed=4 * length * columns,
            transcendentals=2 * pairs * qw // hd,
        ),
        name="attention",
    )(meta, *chunks)


def weight_kernel(owners, at_once, parts, meta, slab_ref, *refs):
    rows_refs = refs[:parts]
    kept, sent, total = refs[parts], refs[parts + 1 : -1], refs[-1]
    my_dp = meta[1]
    first = 0
    for ref in rows_refs:
        width = ref.shape[1]
        total[:, first : first + width] = dot(slab_ref[...], ref[...], TN)
        first += width
    piece = total.shape[0] // owners
    for rel in range(owners):
        rows = pl.ds(pl.multiple_of((my_dp ^ rel) * piece, piece), piece)
        to = slice((rel >> 1) * piece, ((rel >> 1) + 1) * piece)
        if at_once and rel:
            sent[rel - 1][...] = total[rows, :].astype(sent[rel - 1].dtype)
        elif at_once:
            kept[...] = total[rows, :]
        elif rel & 1:
            sent[0][to, :] = total[rows, :].astype(sent[0].dtype)
        else:
            kept[to, :] = total[rows, :]


def weight_part(meta, slab, grads, owners, at_once):
    length, features = slab.shape
    columns = sum(part.shape[1] for part in grads)
    rows = features // owners if at_once else features // 2
    sends = owners - 1 if at_once else 1
    return pl.pallas_call(
        functools.partial(weight_kernel, owners, at_once, len(grads)),
        out_shape=(jax.ShapeDtypeStruct((rows, columns), jnp.float32),)
        + (jax.ShapeDtypeStruct((rows, columns), jnp.bfloat16),) * sends,
        in_specs=[smem()] + [vmem()] * (1 + len(grads)),
        out_specs=(vmem(),) * (1 + sends),
        scratch_shapes=[pltpu.VMEM((features, columns), jnp.float32)],
        compiler_params=kernel_params(),
        cost_estimate=pl.CostEstimate(
            flops=2 * length * features * columns,
            bytes_accessed=2 * length * (features + columns),
            transcendentals=0,
        ),
        name="weight_part",
    )(meta, slab, *grads)


def fold_kernel(piece, kept_ref, arrived_ref, kept, sent):
    for j in range(kept_ref.shape[0] // piece):
        rows = slice(j * piece, (j + 1) * piece)
        total = kept_ref[rows, :] + arrived_ref[rows, :].astype(jnp.float32)
        to = slice((j >> 1) * piece, ((j >> 1) + 1) * piece)
        if j & 1:
            sent[to, :] = total.astype(sent.dtype)
        else:
            kept[to, :] = total


def fold(kept, arrived, piece):
    rows, columns = kept.shape
    return pl.pallas_call(
        functools.partial(fold_kernel, piece),
        out_shape=(
            jax.ShapeDtypeStruct((rows // 2, columns), jnp.float32),
            jax.ShapeDtypeStruct((rows // 2, columns), jnp.bfloat16),
        ),
        in_specs=[vmem()] * 2,
        out_specs=(vmem(),) * 2,
        compiler_params=kernel_params(),
        name="fold",
    )(kept, arrived)


def final_kernel(sizes, *refs):
    out_ref = refs[-1]
    first = at = 0
    for size in sizes:
        total = refs[at][...]
        for ref in refs[at + 1 : at + size]:
            total = total + ref[...].astype(jnp.float32)
        out_ref[:, first : first + total.shape[1]] = total
        first += total.shape[1]
        at += size


def final_sum(groups):
    flat = [array for group in groups for array in group]
    columns = sum(group[0].shape[1] for group in groups)
    return pl.pallas_call(
        functools.partial(final_kernel, [len(group) for group in groups]),
        out_shape=jax.ShapeDtypeStruct((flat[0].shape[0], columns), jnp.float32),
        in_specs=[vmem()] * len(flat),
        out_specs=vmem(),
        compiler_params=kernel_params(),
        name="final_sum",
    )(*flat)


def halved(terms, piece, bit):
    while bit < lax.axis_size("dp"):
        kept, sent = fold(*terms, piece)
        terms = [kept, swap(sent, "dp", bit)]
        bit *= 2
    return terms


def ordered(first, later):
    return lax.optimization_barrier((first, later))


def body(layer_input, query_proj, key_proj, value_proj, out_grad, block_pos, doc_ids):
    dp = lax.axis_size("dp")
    blocks = block_pos.shape[1]
    hd = key_proj.shape[2]
    me = jnp.stack([lax.axis_index("seq"), lax.axis_index("dp")]).astype(jnp.int32)
    meta = jnp.concatenate([me, block_pos[0], doc_ids[0]])
    slab = layer_input[0]

    own = jnp.concatenate([key_proj[0], value_proj[0], query_proj[0], out_grad[0]], axis=1)
    sent = [across(own, step) for step in range(2)]
    sent[0], meta = ordered(sent[0], meta)
    sent.append(across(sent[0], 1))
    chunks = with_other_core([own] + sent)
    *dqs, dk, dv = attention(meta, blocks, hd, chunks, 2)

    halving = 1 < dp <= 8 and dp & (dp - 1) == 0
    grads = [[dk, dv]] + [[dq] for dq in dqs]
    owners = dp if halving else 1
    terms = [weight_part(meta, slab, grad, owners, not halving) for grad in grads]
    terms = terms[1:] + terms[:1]
    if not halving:
        whole = jnp.concatenate([kept for kept, in terms], axis=1)
        return lax.psum_scatter(whole, "dp", scatter_dimension=0, tiled=True)
    terms = [[kept, swap(part, "dp", 1)] for kept, part in terms]
    return final_sum([halved(term, slab.shape[1] // dp, 2) for term in terms])


def solution(mesh):
    placed = (
        P("dp", None, "seq"),
        P("dp", "seq", None),
        P("dp", "seq", None),
        P("dp", "seq", None),
        P("dp", "seq", None),
        P("dp", None),
        P("dp", None),
    )
    return jax.shard_map(
        body, mesh=mesh, in_specs=placed, out_specs=P(("seq", "dp"), None), check_vma=False
    )
```

```python
import functools
import math

import jax
import jax.numpy as jnp
from jax import lax
from jax.experimental import pallas as pl
from jax.experimental.pallas import tpu as pltpu
from jax.sharding import PartitionSpec as P

masked_fill = -1e30
MOST_DOC = 4
TOGETHER = 1
AT_ONCE = {1: (4, 2, 1), 2: (2, 1), 3: (1,), 4: (1,)}
VMEM_LIMIT = 24 * 1024 * 1024

NT = (((1,), (1,)), ((), ()))
NN = (((1,), (0,)), ((), ()))
TN = (((0,), (0,)), ((), ()))


def dot(a, b, dims):
    return lax.dot_general(a, b, dims, preferred_element_type=jnp.float32)


def smem():
    return pl.BlockSpec(memory_space=pltpu.SMEM)


def vmem():
    return pl.BlockSpec(memory_space=pltpu.VMEM)


def kernel_params():
    return pltpu.CompilerParams(vmem_limit_bytes=VMEM_LIMIT)


def swap(x, axis, rel):
    return lax.ppermute(x, axis, [(i, i ^ rel) for i in range(lax.axis_size(axis))])


def routes(shards):
    bits = [1 << b for b in range(1, shards.bit_length() - 1)]
    return bits, bits[::-1]


def across(x, step):
    shards = lax.axis_size("seq")
    even, odd = routes(shards)
    pairs = [(i, i ^ (odd if i & 1 else even)[step]) for i in range(shards)]
    return lax.ppermute(x, "seq", pairs)


def from_chips(x):
    chunks = [x]
    for step in range(len(routes(lax.axis_size("seq"))[0])):
        chunks += [across(chunk, step) for chunk in chunks]
    return chunks


def with_other_core(chunks):
    return [part for chunk in chunks for part in (chunk, swap(chunk, "seq", 1))]


def origin(me, place, shards):
    def offset(order):
        return sum(bit for j, bit in enumerate(order) if (place >> 1) >> j & 1)

    even, odd = (offset(order) for order in routes(shards))
    core = me & 1
    if place & 1:
        return me ^ 1 ^ (odd + (even - odd) * core)
    return me ^ (even + (odd - even) * core)


def hold_kernel(x_ref, out_ref):
    out_ref[...] = x_ref[...]


def held(x):
    return pl.pallas_call(
        hold_kernel,
        out_shape=jax.ShapeDtypeStruct(x.shape, x.dtype),
        in_specs=[vmem()],
        out_specs=vmem(),
        compiler_params=kernel_params(),
        name="held",
    )(x)


def attention_kernel(shards, blocks, heads, hd, scaling, *refs):
    meta = refs[0]
    chunks = refs[1 : 1 + shards]
    grad_chunks = refs[1 + shards : 1 + 2 * shards]
    dq_refs = refs[1 + 2 * shards : -8]
    dk_ref, dv_ref, keys, values, queries, grads, inverse, starts = refs[-8:]
    me = meta[0]
    per_dev = blocks // shards
    span = keys.shape[0] // blocks
    qw = heads * hd

    def document(place):
        return meta[2 + blocks + place]

    def rows_at(first, count):
        return pl.ds(pl.multiple_of(first * span, span), count * span)

    for place in range(shards):
        device = origin(me, place, shards)
        for b in range(per_dev):
            storage = device * per_dev + b
            position = meta[2 + storage]
            inverse[position] = storage
            rows = rows_at(position, 1)
            here = slice(b * span, (b + 1) * span)
            at = 0
            grads[rows, :] = grad_chunks[place][here, :]
            for whole in (keys, values, queries):
                whole[rows, :] = chunks[place][here, at : at + whole.shape[1]]
                at += whole.shape[1]

    def note(state):
        first, counts = state[0], state[1:]
        size = jnp.int32(1)
        for ahead in range(1, MOST_DOC):
            at = jnp.minimum(first + ahead, blocks - 1)
            same = (first + ahead < blocks) & (document(at) == document(first))
            size = size + same.astype(jnp.int32)
        listed = counts[0]
        for n in range(2, MOST_DOC + 1):
            listed = jnp.where(size == n, counts[n - 1], listed)
        starts[(size - 1) * blocks + listed] = first
        counts = tuple(
            count + (size == n + 1).astype(jnp.int32) for n, count in enumerate(counts)
        )
        return (first + size,) + counts

    listed = lax.while_loop(
        lambda state: state[0] < blocks, note, (jnp.int32(0),) * (MOST_DOC + 1)
    )[1:]

    def stacked(ref, first, count):
        return jnp.concatenate(
            [ref[rows_at(first, count), h * hd : (h + 1) * hd] for h in range(heads)], axis=0
        )

    def masked(scores, before, count):
        square = (count * span, heads * count * span)
        key_at = lax.broadcasted_iota(jnp.int32, square, 0)
        query_at = lax.rem(lax.broadcasted_iota(jnp.int32, square, 1), count * span)
        diagonal = jnp.where(key_at <= query_at, scores[before * span :], masked_fill)
        if not before:
            return diagonal
        return jnp.concatenate([scores[: before * span], diagonal], axis=0)

    def step(firsts, size):
        parts = [
            (first, before, min(TOGETHER, size - before))
            for first in firsts
            for before in range(0, size, TOGETHER)
        ]
        q_cats = [stacked(queries, first + before, count) for first, before, count in parts]
        g_cats = [stacked(grads, first + before, count) for first, before, count in parts]
        key_wins = [keys[rows_at(first, before + count), :] for first, before, count in parts]
        value_wins = [values[rows_at(first, before + count), :] for first, before, count in parts]
        scores = [dot(key_win, q_cat, NT) for key_win, q_cat in zip(key_wins, q_cats)]
        dprobs = [dot(value_win, g_cat, NT) for value_win, g_cat in zip(value_wins, g_cats)]
        scores = [masked(s, before, count) for s, (_, before, count) in zip(scores, parts)]
        peaks = [jnp.max(s, axis=0, keepdims=True) for s in scores]
        weights = [
            jnp.exp2((s - peak) * (scaling * math.log2(math.e)))
            for s, peak in zip(scores, peaks)
        ]
        shares = [1.0 / jnp.sum(w, axis=0, keepdims=True) for w in weights]
        probs = [w * share for w, share in zip(weights, shares)]
        probs_b = [p.astype(jnp.bfloat16) for p in probs]
        deltas = [
            jnp.sum(p.astype(jnp.float32) * dp, axis=0, keepdims=True)
            for p, dp in zip(probs_b, dprobs)
        ]
        dscores = [
            (p * (dp - delta)).astype(jnp.bfloat16)
            for p, dp, delta in zip(probs, dprobs, deltas)
        ]
        dks = [dot(ds, q_cat, NN) for ds, q_cat in zip(dscores, q_cats)]
        dvs = [dot(p, g_cat, NN) for p, g_cat in zip(probs_b, g_cats)]
        dqs = [
            (dot(ds, key_win, TN) * scaling).astype(jnp.bfloat16)
            for ds, key_win in zip(dscores, key_wins)
        ]
        for dq, (first, before, count) in zip(dqs, parts):
            for t in range(count):
                at = rows_at(inverse[first + before + t], 1)
                for h in range(heads):
                    start = (h * count + t) * span
                    dq_ref = dq_refs[h * len(dq_refs) // heads]
                    column = h * hd % dq_ref.shape[1]
                    dq_ref[at, column : column + hd] = dq[start : start + span]
        for first in firsts:
            for j in range(size):
                reach = [
                    i
                    for i, (start, before, count) in enumerate(parts)
                    if start is first and before + count > j
                ]
                rows = slice(j * span, (j + 1) * span)
                dk = sum(dks[i][rows] for i in reach) * scaling
                dv = sum(dvs[i][rows] for i in reach)
                at = rows_at(inverse[first + j], 1)
                dk_ref[at, :] = dk.astype(dk_ref.dtype)
                dv_ref[at, :] = dv.astype(dv_ref.dtype)

    for size in range(MOST_DOC, 0, -1):
        done = jnp.int32(0)
        for together in AT_ONCE[size]:
            times = (listed[size - 1] - done) // together

            def some(k, carry, size=size, together=together, done=done):
                at = (size - 1) * blocks + done + k * together
                step([starts[at + d] for d in range(together)], size)
                return carry

            lax.fori_loop(0, times, some, jnp.int32(0))
            done = done + times * together


def attention(meta, blocks, hd, chunks, groups):
    shards = len(chunks) // 2
    tok, columns = chunks[0].shape
    length = tok * shards
    qw = columns - 2 * hd
    outs = (qw // groups,) * groups + (hd, hd)
    pairs = length * length // blocks
    return pl.pallas_call(
        functools.partial(attention_kernel, shards, blocks, qw // hd, hd, hd**-0.5),
        out_shape=tuple(jax.ShapeDtypeStruct((length, width), jnp.bfloat16) for width in outs),
        in_specs=[smem()] + [vmem()] * (2 * shards),
        out_specs=(vmem(),) * len(outs),
        scratch_shapes=[
            pltpu.VMEM((length, hd), jnp.bfloat16),
            pltpu.VMEM((length, hd), jnp.bfloat16),
            pltpu.VMEM((length, qw), jnp.bfloat16),
            pltpu.VMEM((length, qw), jnp.bfloat16),
            pltpu.SMEM((blocks,), jnp.int32),
            pltpu.SMEM((MOST_DOC * blocks,), jnp.int32),
        ],
        compiler_params=kernel_params(),
        cost_estimate=pl.CostEstimate(
            flops=20 * pairs * qw,
            bytes_accessed=4 * length * columns,
            transcendentals=2 * pairs * qw // hd,
        ),
        name="attention",
    )(meta, *chunks)


def weight_kernel(owners, at_once, parts, meta, slab_ref, *refs):
    rows_refs = refs[:parts]
    kept, sent, total = refs[parts], refs[parts + 1 : -1], refs[-1]
    my_dp = meta[1]
    first = 0
    for ref in rows_refs:
        width = ref.shape[1]
        total[:, first : first + width] = dot(slab_ref[...], ref[...], TN)
        first += width
    piece = total.shape[0] // owners
    for rel in range(owners):
        rows = pl.ds(pl.multiple_of((my_dp ^ rel) * piece, piece), piece)
        to = slice((rel >> 1) * piece, ((rel >> 1) + 1) * piece)
        if at_once and rel:
            sent[rel - 1][...] = total[rows, :].astype(sent[rel - 1].dtype)
        elif at_once:
            kept[...] = total[rows, :]
        elif rel & 1:
            sent[0][to, :] = total[rows, :].astype(sent[0].dtype)
        else:
            kept[to, :] = total[rows, :]


def weight_part(meta, slab, grads, owners, at_once):
    length, features = slab.shape
    columns = sum(part.shape[1] for part in grads)
    rows = features // owners if at_once else features // 2
    sends = owners - 1 if at_once else 1
    return pl.pallas_call(
        functools.partial(weight_kernel, owners, at_once, len(grads)),
        out_shape=(jax.ShapeDtypeStruct((rows, columns), jnp.float32),)
        + (jax.ShapeDtypeStruct((rows, columns), jnp.bfloat16),) * sends,
        in_specs=[smem()] + [vmem()] * (1 + len(grads)),
        out_specs=(vmem(),) * (1 + sends),
        scratch_shapes=[pltpu.VMEM((features, columns), jnp.float32)],
        compiler_params=kernel_params(),
        cost_estimate=pl.CostEstimate(
            flops=2 * length * features * columns,
            bytes_accessed=2 * length * (features + columns),
            transcendentals=0,
        ),
        name="weight_part",
    )(meta, slab, *grads)


def fold_kernel(piece, kept_ref, arrived_ref, kept, sent):
    for j in range(kept_ref.shape[0] // piece):
        rows = slice(j * piece, (j + 1) * piece)
        total = kept_ref[rows, :] + arrived_ref[rows, :].astype(jnp.float32)
        to = slice((j >> 1) * piece, ((j >> 1) + 1) * piece)
        if j & 1:
            sent[to, :] = total.astype(sent.dtype)
        else:
            kept[to, :] = total


def fold(kept, arrived, piece):
    rows, columns = kept.shape
    return pl.pallas_call(
        functools.partial(fold_kernel, piece),
        out_shape=(
            jax.ShapeDtypeStruct((rows // 2, columns), jnp.float32),
            jax.ShapeDtypeStruct((rows // 2, columns), jnp.bfloat16),
        ),
        in_specs=[vmem()] * 2,
        out_specs=(vmem(),) * 2,
        compiler_params=kernel_params(),
        name="fold",
    )(kept, arrived)


def final_kernel(sizes, *refs):
    out_ref = refs[-1]
    first = at = 0
    for size in sizes:
        total = refs[at][...]
        for ref in refs[at + 1 : at + size]:
            total = total + ref[...].astype(jnp.float32)
        out_ref[:, first : first + total.shape[1]] = total
        first += total.shape[1]
        at += size


def final_sum(groups):
    flat = [array for group in groups for array in group]
    columns = sum(group[0].shape[1] for group in groups)
    return pl.pallas_call(
        functools.partial(final_kernel, [len(group) for group in groups]),
        out_shape=jax.ShapeDtypeStruct((flat[0].shape[0], columns), jnp.float32),
        in_specs=[vmem()] * len(flat),
        out_specs=vmem(),
        compiler_params=kernel_params(),
        name="final_sum",
    )(*flat)


def halved(terms, piece, bit):
    while bit < lax.axis_size("dp"):
        kept, sent = fold(*terms, piece)
        terms = [kept, swap(sent, "dp", bit)]
        bit *= 2
    return terms


def ordered(first, later):
    return lax.optimization_barrier((first, later))


def body(layer_input, query_proj, key_proj, value_proj, out_grad, block_pos, doc_ids):
    dp = lax.axis_size("dp")
    blocks = block_pos.shape[1]
    hd = key_proj.shape[2]
    me = jnp.stack([lax.axis_index("seq"), lax.axis_index("dp")]).astype(jnp.int32)
    meta = jnp.concatenate([me, block_pos[0], doc_ids[0]])
    slab = layer_input[0]

    own_grad = out_grad[0]
    own = jnp.concatenate([key_proj[0], value_proj[0], query_proj[0]], axis=1)
    grad_sent = across(own_grad, 0)
    sent = across(own, 0)
    grad_sent, (own_grad, own, meta) = ordered(grad_sent, (own_grad, own, meta))
    grad_chunks = [own_grad, grad_sent, across(own_grad, 1), across(grad_sent, 1)]
    chunks = [own, sent, across(own, 1), across(sent, 1)]
    early_grads = with_other_core([held(own_grad)] + grad_chunks[1:3])
    early = with_other_core(chunks[:3])
    (grad_chunks, chunks), (early_grads, early) = ordered(
        (grad_chunks, chunks), (early_grads, early)
    )
    chunks = early + with_other_core(chunks[3:]) + early_grads + with_other_core(grad_chunks[3:])
    *dqs, dk, dv = attention(meta, blocks, hd, chunks, 2)

    halving = 1 < dp <= 8 and dp & (dp - 1) == 0
    grads = [[dk, dv]] + [[dq] for dq in dqs]
    owners = dp if halving else 1
    terms = [weight_part(meta, slab, grad, owners, not halving) for grad in grads]
    terms = terms[1:] + terms[:1]
    if not halving:
        whole = jnp.concatenate([kept for kept, in terms], axis=1)
        return lax.psum_scatter(whole, "dp", scatter_dimension=0, tiled=True)
    terms = [[kept, swap(part, "dp", 1)] for kept, part in terms]
    return final_sum([halved(term, slab.shape[1] // dp, 2) for term in terms])


def solution(mesh):
    placed = (
        P("dp", None, "seq"),
        P("dp", "seq", None),
        P("dp", "seq", None),
        P("dp", "seq", None),
        P("dp", "seq", None),
        P("dp", None),
        P("dp", None),
    )
    return jax.shard_map(
        body, mesh=mesh, in_specs=placed, out_specs=P(("seq", "dp"), None), check_vma=False
    )
```

```python
import functools
import math

import jax
import jax.numpy as jnp
from jax import lax
from jax.experimental import pallas as pl
from jax.experimental.pallas import tpu as pltpu
from jax.sharding import PartitionSpec as P

masked_fill = -1e30
MOST_DOC = 4
TOGETHER = 1
AT_ONCE = {1: (4, 2, 1), 2: (2, 1), 3: (1,), 4: (1,)}
VMEM_LIMIT = 16 * 1024 * 1024

NT = (((1,), (1,)), ((), ()))
NN = (((1,), (0,)), ((), ()))
TN = (((0,), (0,)), ((), ()))


def dot(a, b, dims):
    return lax.dot_general(a, b, dims, preferred_element_type=jnp.float32)


def smem():
    return pl.BlockSpec(memory_space=pltpu.SMEM)


def vmem():
    return pl.BlockSpec(memory_space=pltpu.VMEM)


def kernel_params():
    return pltpu.CompilerParams(vmem_limit_bytes=VMEM_LIMIT)


def swap(x, axis, rel):
    return lax.ppermute(x, axis, [(i, i ^ rel) for i in range(lax.axis_size(axis))])


def routes(shards):
    bits = [1 << b for b in range(1, shards.bit_length() - 1)]
    return bits, bits[::-1]


def across(x, step):
    shards = lax.axis_size("seq")
    even, odd = routes(shards)
    pairs = [(i, i ^ (odd if i & 1 else even)[step]) for i in range(shards)]
    return lax.ppermute(x, "seq", pairs)


def from_chips(x):
    chunks = [x]
    for step in range(len(routes(lax.axis_size("seq"))[0])):
        chunks += [across(chunk, step) for chunk in chunks]
    return chunks


def with_other_core(chunks):
    return [part for chunk in chunks for part in (chunk, swap(chunk, "seq", 1))]


def origin(me, place, shards):
    def offset(order):
        return sum(bit for j, bit in enumerate(order) if (place >> 1) >> j & 1)

    even, odd = (offset(order) for order in routes(shards))
    core = me & 1
    if place & 1:
        return me ^ 1 ^ (odd + (even - odd) * core)
    return me ^ (even + (odd - even) * core)


def hold_kernel(x_ref, out_ref):
    out_ref[...] = x_ref[...]


def held(x):
    return pl.pallas_call(
        hold_kernel,
        out_shape=jax.ShapeDtypeStruct(x.shape, x.dtype),
        in_specs=[vmem()],
        out_specs=vmem(),
        compiler_params=kernel_params(),
        name="held",
    )(x)


def attention_kernel(shards, blocks, heads, hd, scaling, *refs):
    meta = refs[0]
    chunks = refs[1 : 1 + shards]
    grad_chunks = refs[1 + shards : 1 + 2 * shards]
    dq_refs = refs[1 + 2 * shards : -8]
    dk_ref, dv_ref, keys, values, queries, grads, inverse, starts = refs[-8:]
    me = meta[0]
    per_dev = blocks // shards
    span = keys.shape[0] // blocks
    qw = heads * hd

    def document(place):
        return meta[2 + blocks + place]

    def rows_at(first, count):
        return pl.ds(pl.multiple_of(first * span, span), count * span)

    for place in range(shards):
        device = origin(me, place, shards)
        for b in range(per_dev):
            storage = device * per_dev + b
            position = meta[2 + storage]
            inverse[position] = storage
            rows = rows_at(position, 1)
            here = slice(b * span, (b + 1) * span)
            at = 0
            grads[rows, :] = grad_chunks[place][here, :]
            for whole in (keys, values, queries):
                whole[rows, :] = chunks[place][here, at : at + whole.shape[1]]
                at += whole.shape[1]

    def note(state):
        first, counts = state[0], state[1:]
        size = jnp.int32(1)
        for ahead in range(1, MOST_DOC):
            at = jnp.minimum(first + ahead, blocks - 1)
            same = (first + ahead < blocks) & (document(at) == document(first))
            size = size + same.astype(jnp.int32)
        listed = counts[0]
        for n in range(2, MOST_DOC + 1):
            listed = jnp.where(size == n, counts[n - 1], listed)
        starts[(size - 1) * blocks + listed] = first
        counts = tuple(
            count + (size == n + 1).astype(jnp.int32) for n, count in enumerate(counts)
        )
        return (first + size,) + counts

    listed = lax.while_loop(
        lambda state: state[0] < blocks, note, (jnp.int32(0),) * (MOST_DOC + 1)
    )[1:]

    def stacked(ref, first, count):
        return jnp.concatenate(
            [ref[rows_at(first, count), h * hd : (h + 1) * hd] for h in range(heads)], axis=0
        )

    def masked(scores, before, count):
        square = (count * span, heads * count * span)
        key_at = lax.broadcasted_iota(jnp.int32, square, 0)
        query_at = lax.rem(lax.broadcasted_iota(jnp.int32, square, 1), count * span)
        diagonal = jnp.where(key_at <= query_at, scores[before * span :], masked_fill)
        if not before:
            return diagonal
        return jnp.concatenate([scores[: before * span], diagonal], axis=0)

    def step(firsts, size):
        parts = [
            (first, before, min(TOGETHER, size - before))
            for first in firsts
            for before in range(0, size, TOGETHER)
        ]
        q_cats = [stacked(queries, first + before, count) for first, before, count in parts]
        g_cats = [stacked(grads, first + before, count) for first, before, count in parts]
        key_wins = [keys[rows_at(first, before + count), :] for first, before, count in parts]
        value_wins = [values[rows_at(first, before + count), :] for first, before, count in parts]
        scores = [dot(key_win, q_cat, NT) for key_win, q_cat in zip(key_wins, q_cats)]
        dprobs = [dot(value_win, g_cat, NT) for value_win, g_cat in zip(value_wins, g_cats)]
        scores = [masked(s, before, count) for s, (_, before, count) in zip(scores, parts)]
        peaks = [jnp.max(s, axis=0, keepdims=True) for s in scores]
        weights = [
            jnp.exp2((s - peak) * (scaling * math.log2(math.e)))
            for s, peak in zip(scores, peaks)
        ]
        shares = [1.0 / jnp.sum(w, axis=0, keepdims=True) for w in weights]
        probs = [w * share for w, share in zip(weights, shares)]
        probs_b = [p.astype(jnp.bfloat16) for p in probs]
        deltas = [
            jnp.sum(p.astype(jnp.float32) * dp, axis=0, keepdims=True)
            for p, dp in zip(probs_b, dprobs)
        ]
        dscores = [
            (p * (dp - delta)).astype(jnp.bfloat16)
            for p, dp, delta in zip(probs, dprobs, deltas)
        ]
        dks = [dot(ds, q_cat, NN) for ds, q_cat in zip(dscores, q_cats)]
        dvs = [dot(p, g_cat, NN) for p, g_cat in zip(probs_b, g_cats)]
        dqs = [
            (dot(ds, key_win, TN) * scaling).astype(jnp.bfloat16)
            for ds, key_win in zip(dscores, key_wins)
        ]
        for dq, (first, before, count) in zip(dqs, parts):
            for t in range(count):
                at = rows_at(inverse[first + before + t], 1)
                for h in range(heads):
                    start = (h * count + t) * span
                    dq_ref = dq_refs[h * len(dq_refs) // heads]
                    column = h * hd % dq_ref.shape[1]
                    dq_ref[at, column : column + hd] = dq[start : start + span]
        for first in firsts:
            for j in range(size):
                reach = [
                    i
                    for i, (start, before, count) in enumerate(parts)
                    if start is first and before + count > j
                ]
                rows = slice(j * span, (j + 1) * span)
                dk = sum(dks[i][rows] for i in reach) * scaling
                dv = sum(dvs[i][rows] for i in reach)
                at = rows_at(inverse[first + j], 1)
                dk_ref[at, :] = dk.astype(dk_ref.dtype)
                dv_ref[at, :] = dv.astype(dv_ref.dtype)

    for size in range(MOST_DOC, 0, -1):
        done = jnp.int32(0)
        for together in AT_ONCE[size]:
            times = (listed[size - 1] - done) // together

            def some(k, carry, size=size, together=together, done=done):
                at = (size - 1) * blocks + done + k * together
                step([starts[at + d] for d in range(together)], size)
                return carry

            lax.fori_loop(0, times, some, jnp.int32(0))
            done = done + times * together


def attention(meta, blocks, hd, chunks, groups):
    shards = len(chunks) // 2
    tok, columns = chunks[0].shape
    length = tok * shards
    qw = columns - 2 * hd
    outs = (qw // groups,) * groups + (hd, hd)
    pairs = length * length // blocks
    return pl.pallas_call(
        functools.partial(attention_kernel, shards, blocks, qw // hd, hd, hd**-0.5),
        out_shape=tuple(jax.ShapeDtypeStruct((length, width), jnp.bfloat16) for width in outs),
        in_specs=[smem()] + [vmem()] * (2 * shards),
        out_specs=(vmem(),) * len(outs),
        scratch_shapes=[
            pltpu.VMEM((length, hd), jnp.bfloat16),
            pltpu.VMEM((length, hd), jnp.bfloat16),
            pltpu.VMEM((length, qw), jnp.bfloat16),
            pltpu.VMEM((length, qw), jnp.bfloat16),
            pltpu.SMEM((blocks,), jnp.int32),
            pltpu.SMEM((MOST_DOC * blocks,), jnp.int32),
        ],
        compiler_params=kernel_params(),
        cost_estimate=pl.CostEstimate(
            flops=20 * pairs * qw,
            bytes_accessed=4 * length * columns,
            transcendentals=2 * pairs * qw // hd,
        ),
        name="attention",
    )(meta, *chunks)


def weight_kernel(owners, at_once, parts, meta, slab_ref, *refs):
    rows_refs = refs[:parts]
    kept, sent = refs[parts], refs[parts + 1 :]
    my_dp = meta[1]
    piece = slab_ref.shape[1] // owners
    for rel in range(owners):
        features = pl.ds(pl.multiple_of((my_dp ^ rel) * piece, piece), piece)
        to = slice((rel >> 1) * piece, ((rel >> 1) + 1) * piece)
        if at_once:
            ref, to = (sent[rel - 1] if rel else kept), slice(0, piece)
        else:
            ref = sent[0] if rel & 1 else kept
        first = 0
        for rows in rows_refs:
            width = rows.shape[1]
            total = dot(slab_ref[:, features], rows[...], TN)
            ref[to, first : first + width] = total.astype(ref.dtype)
            first += width


def weight_part(meta, slab, grads, owners, at_once):
    length, features = slab.shape
    columns = sum(part.shape[1] for part in grads)
    rows = features // owners if at_once else features // 2
    sends = owners - 1 if at_once else 1
    return pl.pallas_call(
        functools.partial(weight_kernel, owners, at_once, len(grads)),
        out_shape=(jax.ShapeDtypeStruct((rows, columns), jnp.float32),)
        + (jax.ShapeDtypeStruct((rows, columns), jnp.bfloat16),) * sends,
        in_specs=[smem()] + [vmem()] * (1 + len(grads)),
        out_specs=(vmem(),) * (1 + sends),
        compiler_params=kernel_params(),
        cost_estimate=pl.CostEstimate(
            flops=2 * length * features * columns,
            bytes_accessed=2 * length * (features + columns),
            transcendentals=0,
        ),
        name="weight_part",
    )(meta, slab, *grads)


def fold_kernel(piece, kept_ref, arrived_ref, kept, sent):
    for j in range(kept_ref.shape[0] // piece):
        rows = slice(j * piece, (j + 1) * piece)
        total = kept_ref[rows, :] + arrived_ref[rows, :].astype(jnp.float32)
        to = slice((j >> 1) * piece, ((j >> 1) + 1) * piece)
        if j & 1:
            sent[to, :] = total.astype(sent.dtype)
        else:
            kept[to, :] = total


def fold(kept, arrived, piece):
    rows, columns = kept.shape
    return pl.pallas_call(
        functools.partial(fold_kernel, piece),
        out_shape=(
            jax.ShapeDtypeStruct((rows // 2, columns), jnp.float32),
            jax.ShapeDtypeStruct((rows // 2, columns), jnp.bfloat16),
        ),
        in_specs=[vmem()] * 2,
        out_specs=(vmem(),) * 2,
        compiler_params=kernel_params(),
        name="fold",
    )(kept, arrived)


def final_kernel(sizes, *refs):
    out_ref = refs[-1]
    first = at = 0
    for size in sizes:
        total = refs[at][...]
        for ref in refs[at + 1 : at + size]:
            total = total + ref[...].astype(jnp.float32)
        out_ref[:, first : first + total.shape[1]] = total
        first += total.shape[1]
        at += size


def final_sum(groups):
    flat = [array for group in groups for array in group]
    columns = sum(group[0].shape[1] for group in groups)
    return pl.pallas_call(
        functools.partial(final_kernel, [len(group) for group in groups]),
        out_shape=jax.ShapeDtypeStruct((flat[0].shape[0], columns), jnp.float32),
        in_specs=[vmem()] * len(flat),
        out_specs=vmem(),
        compiler_params=kernel_params(),
        name="final_sum",
    )(*flat)


def halved(terms, piece, bit):
    while bit < lax.axis_size("dp"):
        kept, sent = fold(*terms, piece)
        terms = [kept, swap(sent, "dp", bit)]
        bit *= 2
    return terms


def ordered(first, later):
    return lax.optimization_barrier((first, later))


def body(layer_input, query_proj, key_proj, value_proj, out_grad, block_pos, doc_ids):
    dp = lax.axis_size("dp")
    blocks = block_pos.shape[1]
    hd = key_proj.shape[2]
    me = jnp.stack([lax.axis_index("seq"), lax.axis_index("dp")]).astype(jnp.int32)
    meta = jnp.concatenate([me, block_pos[0], doc_ids[0]])
    slab = layer_input[0]

    own_grad = out_grad[0]
    own = jnp.concatenate([key_proj[0], value_proj[0], query_proj[0]], axis=1)
    grad_sent = across(own_grad, 0)
    sent = across(own, 0)
    grad_sent, (own_grad, own, meta) = ordered(grad_sent, (own_grad, own, meta))
    grad_chunks = [own_grad, grad_sent, across(own_grad, 1), across(grad_sent, 1)]
    chunks = [own, sent, across(own, 1), across(sent, 1)]
    early_grads = with_other_core([held(own_grad)] + grad_chunks[1:3])
    early = with_other_core(chunks[:3])
    (grad_chunks, chunks), (early_grads, early) = ordered(
        (grad_chunks, chunks), (early_grads, early)
    )
    chunks = early + with_other_core(chunks[3:]) + early_grads + with_other_core(grad_chunks[3:])
    *dqs, dk, dv = attention(meta, blocks, hd, chunks, 2)

    halving = 1 < dp <= 8 and dp & (dp - 1) == 0
    grads = [[dk, dv]] + [[dq] for dq in dqs]
    owners = dp if halving else 1
    terms = [weight_part(meta, slab, grad, owners, not halving) for grad in grads]
    terms = terms[1:] + terms[:1]
    if not halving:
        whole = jnp.concatenate([kept for kept, in terms], axis=1)
        return lax.psum_scatter(whole, "dp", scatter_dimension=0, tiled=True)
    terms = [[kept, swap(part, "dp", 1)] for kept, part in terms]
    return final_sum([halved(term, slab.shape[1] // dp, 2) for term in terms])


def solution(mesh):
    placed = (
        P("dp", None, "seq"),
        P("dp", "seq", None),
        P("dp", "seq", None),
        P("dp", "seq", None),
        P("dp", "seq", None),
        P("dp", None),
        P("dp", None),
    )
    return jax.shard_map(
        body, mesh=mesh, in_specs=placed, out_specs=P(("seq", "dp"), None), check_vma=False
    )
```
